512 devices in a mesh: row: 16 (over x, y), col: 32 (over z, core).
Axes of the slice: x: 4, y: 4, z: 16, core: 2. Of those that a mesh axis runs over, the one named last changes fastest.
Arguments:
- design: float32 [4096, 122880], P('row', 'col')
- targets: float32 [64, 4096], P(None, 'row')
Outputs:
- solution: float32 [64, 122880], P(None, 'col')
All inputs are finite; a program needn't handle non-finite values.
Results may differ from the reference program's by a relative error of at most 0.0001.
Values sent between devices are 32-bit elements; how exact they have to be, the bound alone decides.
A program may use at most 64 MiB of HBM per device.

```python
import math
import jax
import jax.numpy as jnp
from jax import lax

PARAMS = 122880
SETS = 64
ITERS = 2
ROWS = 4096


def draw_design(key, part):
    key = jax.random.fold_in(key, 11)
    first_key, second_key = jax.random.split(key)
    base = jax.random.normal(first_key, (ROWS, PARAMS), jnp.float32)
    scales = jnp.exp(jax.random.uniform(second_key, (1, PARAMS), jnp.float32, -0.693, 0.693))
    return base * scales / math.sqrt(PARAMS)


def draw_targets(key, part):
    key = jax.random.fold_in(key, 23)
    first_key, second_key, third_key = jax.random.split(key, 3)
    sets_scale = jnp.exp(jax.random.uniform(third_key, (SETS, 1), jnp.float32, -0.7, 0.7))
    base = jax.random.normal(first_key, (SETS, ROWS), jnp.float32)
    row_scale = jnp.exp(jax.random.uniform(second_key, (1, ROWS), jnp.float32, 0.0, 2.3026))
    return base * row_scale * sets_scale


def setup_inputs(seed: int = 0) -> dict:
    splits = jax.random.split(jax.random.key(seed), 3)
    return {
        "design": draw_design(jax.random.fold_in(splits[2], 71), 0),
        "targets": draw_targets(jax.random.fold_in(splits[2], 71), 0),
    }


def reference(design, targets):
    highest = lax.Precision.HIGHEST

    def back_product(vector):
        return jnp.dot(vector, design, precision=highest, preferred_element_type=jnp.float32)

    def forward_product(vector):
        return lax.dot_general(vector, design, (((1,), (1,)), ((), ())), precision=highest, preferred_element_type=jnp.float32)

    def row_norms(matrix):
        return jnp.sqrt(lax.optimization_barrier(jnp.sum(matrix * matrix, axis=1)))
    u_norm = row_norms(targets)
    left_vec = targets / u_norm[:, None]
    right_raw = back_product(left_vec)
    v_norm = row_norms(right_raw)
    right_vec = right_raw / v_norm[:, None]
    direction = right_vec
    solution = jnp.zeros_like(right_vec)
    phi_bar = u_norm
    rho_bar = v_norm
    for iteration in range(ITERS):
        final = iteration + 1 == ITERS
        left_raw = forward_product(right_vec) - v_norm[:, None] * left_vec
        u_norm = row_norms(left_raw)
        left_vec = left_raw / u_norm[:, None]
        if not final:
            right_raw = back_product(left_vec) - u_norm[:, None] * right_vec
            v_norm = row_norms(right_raw)
            right_vec = right_raw / v_norm[:, None]
        rho_value = jnp.sqrt(rho_bar * rho_bar + u_norm * u_norm)
        cosine = rho_bar / rho_value
        sine_value = u_norm / rho_value
        phi_value = cosine * phi_bar
        phi_bar = sine_value * phi_bar
        solution = solution + (phi_value / rho_value)[:, None] * direction
        if not final:
            rho_bar = -cosine * v_norm
            direction = right_vec - (sine_value * v_norm / rho_value)[:, None] * direction
    return solution
```

```python
import jax
import jax.numpy as jnp
from jax import lax
from jax.experimental import pallas as pl
from jax.experimental.pallas import tpu as pltpu
from jax.sharding import PartitionSpec as P

MESH = pl.DeviceIdType.MESH
F32 = jnp.float32
BF16 = jnp.bfloat16
SETS = 64
DEPTH = 256
COLS = 3840
TILES = 15
STEPS = COLS // DEPTH


def split(x):
    high = x.astype(BF16)
    low = (x - high.astype(F32)).astype(BF16)
    return high, low


def lane_sum(x):
    return jnp.broadcast_to(jnp.sum(x, axis=-1, keepdims=True), x.shape)


def kernel(
    design, targets, out,
    raw, high, low, partial, arrived, right, units, line_out, line_in, left,
    row_norm, small_src, small_core, small_xy, small_z, tile_core, coef,
    load_sem, send_sem, recv_sem,
):
    me = lax.axis_index("row")
    col = lax.axis_index("col")
    depth_z = col // 2
    core = col % 2
    group = lax.rem(me, 8)
    line_group = lax.rem(depth_z, 8)

    plane = [{"row": lax.rem(me + k, 16), "col": col} for k in range(1, 16)]
    line = [{"row": me, "col": lax.rem(col + 2 * k, 32)} for k in range(1, 16)]
    twin = {"row": me, "col": depth_z * 2 + 1 - core}

    def send(src, dst, index, to):
        pltpu.make_async_remote_copy(
            src_ref=src, dst_ref=dst, send_sem=send_sem.at[index], recv_sem=recv_sem.at[index],
            device_id=to, device_id_type=MESH,
        ).start()

    def arrive(ref, index):
        pltpu.make_async_copy(ref, ref, recv_sem.at[index]).wait()

    def sent(ref, index):
        pltpu.make_async_copy(ref, ref, send_sem.at[index]).wait()

    def load(k):
        where = pl.ds(k * DEPTH, DEPTH)
        return pltpu.make_async_copy(design.at[:, where], raw.at[:, where], load_sem.at[k])

    for k in range(STEPS):
        load(k).start()
    barrier = pltpu.get_barrier_semaphore()
    for to in plane + line + [twin]:
        pl.semaphore_signal(barrier, inc=1, device_id=to, device_id_type=MESH)

    sets_row = lax.broadcasted_iota(jnp.int32, (SETS, 128), 0)
    sets_lane = lax.broadcasted_iota(jnp.int32, (SETS, 128), 1)
    diagonal = sets_row == sets_lane
    b = targets[...]
    squares = jnp.sum(b * b, axis=1, keepdims=True)
    as_row = jnp.sum(jnp.where(diagonal, jnp.broadcast_to(squares, (SETS, 128)), 0.0), axis=0, keepdims=True)
    row_norm[me] = jnp.broadcast_to(as_row, (8, 128))
    pl.semaphore_wait(barrier, 31)
    for to in plane:
        send(row_norm.at[me], row_norm.at[me], 0, to)

    for k in range(STEPS):
        load(k).wait()
        where = pl.ds(k * DEPTH, DEPTH)
        d_high, d_low = split(raw[:, where])
        high[:, where] = d_high
        low[:, where] = d_low

    arrive(row_norm.at[pl.ds(0, 15)], 0)
    sent(row_norm.at[pl.ds(0, 15)], 0)
    total = row_norm[0]
    for k in range(1, 16):
        total = total + row_norm[k]
    b_norm = jnp.sum(jnp.where(diagonal, jnp.broadcast_to(total[:1], (SETS, 128)), 0.0), axis=1, keepdims=True)
    b_norm = jnp.sqrt(jnp.broadcast_to(b_norm, (SETS, 128)))
    u_now = [b[:, :128] / b_norm, b[:, 128:] / b_norm]
    for half in range(2):
        units[pl.ds(8 * half, 8)] = u_now[half].reshape(8, 8, 128)

    def back(halves, turn):
        x_high, x_low = split(jnp.concatenate(halves, axis=1))
        both = jnp.concatenate([x_high, x_low], axis=0)
        for k in range(STEPS):
            where = pl.ds(k * DEPTH, DEPTH)
            first = jnp.dot(both, high[:, where], preferred_element_type=F32)
            second = jnp.dot(x_high, low[:, where], preferred_element_type=F32)
            result = first[:SETS] + (first[SETS:] + second)
            for i in range(2):
                h, j = divmod(2 * k + i, TILES)
                partial[pl.ds(8 * h, 8), j] = result[:, 128 * i:128 * (i + 1)].reshape(8, 8, 128)
        index = 1 + turn
        for to in plane:
            send(partial.at[to["row"]], arrived.at[turn, me], index, to)
        arrived[turn, me] = partial[me]
        arrive(arrived.at[turn, pl.ds(0, 15)], index)
        sent(arrived.at[turn, pl.ds(0, 15)], index)
        total = arrived[turn, 0]
        for k in range(1, 16):
            total = total + arrived[turn, k]
        return total

    def gather(piece, turn):
        right[turn, me] = piece
        index = 3 + turn
        for to in plane:
            send(right.at[turn, me], right.at[turn, me], index, to)
        base = 5 + 3 * turn
        small_z[turn, depth_z] = lane_sum(jnp.sum(piece * piece, axis=0))
        for to in line:
            send(small_z.at[turn, depth_z], small_z.at[turn, depth_z], base, to)
        arrive(small_z.at[turn, pl.ds(0, 15)], base)
        sent(small_z.at[turn, pl.ds(0, 15)], base)
        total = small_z[turn, 0]
        for k in range(1, 16):
            total = total + small_z[turn, k]
        small_src[turn] = total
        send(small_src.at[turn], small_core.at[turn], base + 1, twin)
        arrive(small_core.at[turn], base + 1)
        sent(small_core.at[turn], base + 1)
        small_xy[turn, me] = total + small_core[turn]
        for to in plane:
            send(small_xy.at[turn, me], small_xy.at[turn, me], base + 2, to)
        arrive(right.at[turn, pl.ds(0, 15)], index)
        sent(right.at[turn, pl.ds(0, 15)], index)

    def forward(turn):
        base = 5 + 3 * turn
        slabs = []
        for j in range(2 * TILES):
            h, i = divmod(j, TILES)
            slabs.append((pl.ds(8 * h, 8), i))
        squares = jnp.zeros((8, 8, 128), F32)
        for h, i in slabs:
            v = right[turn, h, i]
            squares = squares + v * v
        own = jnp.sqrt(lane_sum(squares))
        own = jnp.where(own > 0.0, own, 1.0)
        inverse = 1.0 / own
        first = jnp.zeros((2 * SETS, DEPTH), F32)
        second = jnp.zeros((SETS, DEPTH), F32)
        contract = (((1,), (1,)), ((), ()))
        for k in range(STEPS):
            where = pl.ds(k * DEPTH, DEPTH)
            w = [(right[turn, h, i] * inverse).reshape(SETS, 128) for h, i in slabs[2 * k:2 * k + 2]]
            w_high, w_low = split(jnp.concatenate(w, axis=1))
            both = jnp.concatenate([w_high, w_low], axis=0)
            first = first + lax.dot_general(both, high[:, where], contract, preferred_element_type=F32)
            second = second + lax.dot_general(w_high, low[:, where], contract, preferred_element_type=F32)
        result = first[:SETS] + (first[SETS:] + second)
        arrive(small_xy.at[turn, pl.ds(0, 15)], base + 2)
        sent(small_xy.at[turn, pl.ds(0, 15)], base + 2)
        v_norm = jnp.sqrt(small_xy[turn, pl.ds(0, 8)] + small_xy[turn, pl.ds(8, 8)])
        scale = own / v_norm
        for half in range(2):
            line_out[turn, pl.ds(8 * half, 8)] = result[:, 128 * half:128 * (half + 1)].reshape(8, 8, 128) * scale
        index = 11 + 2 * turn
        for to in line:
            send(line_out.at[turn, to["col"] // 2], line_in.at[turn, depth_z], index, to)
        line_in[turn, depth_z] = line_out[turn, depth_z]
        arrive(line_in.at[turn, pl.ds(0, 15)], index)
        sent(line_in.at[turn, pl.ds(0, 15)], index)
        total = line_in[turn, 0]
        for k in range(1, 16):
            total = total + line_in[turn, k]
        small_src[2 + turn] = total
        send(small_src.at[2 + turn], tile_core.at[turn], index + 1, twin)
        arrive(tile_core.at[turn], index + 1)
        sent(tile_core.at[turn], index + 1)
        return total + tile_core[turn], v_norm

    def start_norm(tile, turn):
        index = 15 + 2 * turn
        small_xy[2 + turn, me] = lane_sum(tile * tile)
        for to in plane:
            send(small_xy.at[2 + turn, me], small_xy.at[2 + turn, me], index, to)

    def middle_norm(turn):
        index = 15 + 2 * turn
        arrive(small_xy.at[2 + turn, pl.ds(0, 15)], index)
        sent(small_xy.at[2 + turn, pl.ds(0, 15)], index)
        total = small_xy[2 + turn, 0]
        for k in range(1, 16):
            total = total + small_xy[2 + turn, k]
        small_z[2 + turn, depth_z] = total
        for to in line:
            send(small_z.at[2 + turn, depth_z], small_z.at[2 + turn, depth_z], index + 1, to)

    def end_norm(turn):
        index = 15 + 2 * turn
        arrive(small_z.at[2 + turn, pl.ds(0, 15)], index + 1)
        sent(small_z.at[2 + turn, pl.ds(0, 15)], index + 1)
        return jnp.sqrt(small_z[2 + turn, pl.ds(0, 8)] + small_z[2 + turn, pl.ds(8, 8)])

    piece = back(u_now, 0)
    gather(piece, 0)
    tile, v_first = forward(0)
    coef[0] = v_first
    tile = tile - coef[0, line_group] * units[depth_z]
    start_norm(tile, 0)
    left[depth_z] = tile
    for to in line:
        send(left.at[depth_z], left.at[depth_z], 19, to)
    middle_norm(0)
    arrive(left.at[pl.ds(0, 15)], 19)
    sent(left.at[pl.ds(0, 15)], 19)
    halves = [(left[pl.ds(8 * half, 8)] / v_first).reshape(SETS, 128) for half in range(2)]
    piece = back(halves, 1)
    u_first = end_norm(0)
    coef[1] = u_first
    v_own, u_own = coef[0, group], coef[1, group]
    piece = piece * (v_own / u_own) - right[0, me] * (u_own / v_own)
    gather(piece, 1)
    tile, v_second = forward(1)
    coef[2] = v_second
    tile = tile - coef[2, line_group] * (left[depth_z] / coef[1, line_group])
    start_norm(tile, 1)
    middle_norm(1)
    u_second = end_norm(1)

    phi_bar = b_norm.reshape(8, 8, 128)
    rho = jnp.sqrt(v_first * v_first + u_first * u_first)
    cosine = v_first / rho
    sine = u_first / rho
    step = cosine * phi_bar / rho
    phi_bar = sine * phi_bar
    rho_bar = -cosine * v_second
    turn_back = sine * v_second / rho
    rho = jnp.sqrt(rho_bar * rho_bar + u_second * u_second)
    step_second = (rho_bar / rho) * phi_bar / rho
    for_first = (step - step_second * turn_back) / v_first
    for_second = step_second / v_second
    for j in range(2 * TILES):
        h, i = divmod(j, TILES)
        h = pl.ds(8 * h, 8)
        value = right[0, h, i] * for_first + right[1, h, i] * for_second
        out[:, pl.ds(128 * j, 128)] = value.reshape(SETS, 128)


def local(design, targets):
    tile = (8, 128)
    return pl.pallas_call(
        kernel,
        out_shape=jax.ShapeDtypeStruct((SETS, COLS), F32),
        in_specs=[pl.BlockSpec(memory_space=pl.ANY), pl.BlockSpec(memory_space=pltpu.VMEM)],
        out_specs=pl.BlockSpec(memory_space=pltpu.VMEM),
        scratch_shapes=[
            pltpu.VMEM((DEPTH, COLS), F32),
            pltpu.VMEM((DEPTH, COLS), BF16),
            pltpu.VMEM((DEPTH, COLS), BF16),
            pltpu.VMEM((16, TILES) + tile, F32),
            pltpu.VMEM((2, 16, TILES) + tile, F32),
            pltpu.VMEM((2, 16, TILES) + tile, F32),
            pltpu.VMEM((16,) + tile, F32),
            pltpu.VMEM((2, 16) + tile, F32),
            pltpu.VMEM((2, 16) + tile, F32),
            pltpu.VMEM((16,) + tile, F32),
            pltpu.VMEM((16,) + tile, F32),
            pltpu.VMEM((4,) + tile, F32),
            pltpu.VMEM((2,) + tile, F32),
            pltpu.VMEM((4, 16) + tile, F32),
            pltpu.VMEM((4, 16) + tile, F32),
            pltpu.VMEM((2,) + tile, F32),
            pltpu.VMEM((3, 8) + tile, F32),
            pltpu.SemaphoreType.DMA((STEPS,)),
            pltpu.SemaphoreType.DMA((20,)),
            pltpu.SemaphoreType.DMA((20,)),
        ],
        compiler_params=pltpu.CompilerParams(
            collective_id=0, has_side_effects=True, vmem_limit_bytes=48 << 20
        ),
    )(design, targets)


def solution(mesh):
    in_specs = (P("row", "col"), P(None, "row"))
    return jax.shard_map(local, mesh=mesh, in_specs=in_specs, out_specs=P(None, "col"), check_vma=False)
```

```python
import jax
import jax.numpy as jnp
from jax import lax
from jax.experimental import pallas as pl
from jax.experimental.pallas import tpu as pltpu
from jax.sharding import PartitionSpec as P

MESH = pl.DeviceIdType.MESH
F32 = jnp.float32
BF16 = jnp.bfloat16
SETS = 64
HALF = 32
DEPTH = 256
COLS = 3840
TILES = 15
STEPS = COLS // DEPTH
FAR_FIRST = [(2, 2), (2, 1), (2, 3), (1, 2), (3, 2), (2, 0), (0, 2), (1, 1), (3, 3), (1, 3), (3, 1), (0, 1), (0, 3), (1, 0), (3, 0)]
LINE_EVEN = [8, 6, 10, 4, 12, 2, 14, 0]
LINE_ODD = [7, 9, 5, 11, 3, 13, 1, 15]


def split(x):
    high = x.astype(BF16)
    low = (x - high.astype(F32)).astype(BF16)
    return high, low


def lane_sum(x):
    return jnp.broadcast_to(jnp.sum(x, axis=-1, keepdims=True), x.shape)


def as_row(column):
    at = lax.broadcasted_iota(jnp.int32, (HALF, 128), 0) == lax.broadcasted_iota(jnp.int32, (HALF, 128), 1)
    return jnp.sum(jnp.where(at, column, 0.0), axis=0, keepdims=True)


def as_column(row):
    at = lax.broadcasted_iota(jnp.int32, (HALF, 128), 0) == lax.broadcasted_iota(jnp.int32, (HALF, 128), 1)
    return lane_sum(jnp.where(at, jnp.broadcast_to(row, (HALF, 128)), 0.0)).reshape(4, 8, 128)


def as_tile(row, group):
    sets = lax.broadcasted_iota(jnp.int32, (8, 128), 0) + 8 * group
    at = sets == lax.broadcasted_iota(jnp.int32, (8, 128), 1)
    return lane_sum(jnp.where(at, jnp.broadcast_to(row, (8, 128)), 0.0))


def positive(x):
    return jnp.where(x > 0.0, x, 1.0)


def kernel(
    design, targets, out,
    raw, high, low, base, partial, first_in, second_out, second_in, right, x_row, z_row, twin_out, twin_in, line_out, line_in,
    tile_out, tile_in, left, v_coef, u_coef, end_xy, end_z,
    load_sem, send_sem, recv_sem,
):
    me = lax.axis_index("row")
    col = lax.axis_index("col")
    x, y = me // 4, lax.rem(me, 4)
    z, core = col // 2, lax.rem(col, 2)
    z_parity = lax.rem(z, 2)
    my_tile = z_parity * 8 + z // 2
    tile_group = lax.rem(z // 2, 4)

    def in_plane(dx, dy):
        return lax.rem(x + dx, 4), lax.rem(y + dy, 4)

    def plane_id(tx, ty):
        return {"row": tx * 4 + ty, "col": col}

    plane = [plane_id(*in_plane(*d)) for d in FAR_FIRST]
    line = [
        {"row": me, "col": lax.rem(col + 2 * d, 32)}
        for d in (8, 7, 9, 6, 10, 5, 11, 4, 12, 3, 13, 2, 14, 1, 15)
    ]
    twin = {"row": me, "col": 2 * z + 1 - core}
    waits = []

    def send(src, dst, index, to):
        pltpu.make_async_remote_copy(
            src_ref=src, dst_ref=dst, send_sem=send_sem.at[index], recv_sem=recv_sem.at[index],
            device_id=to, device_id_type=MESH,
        ).start()

    def arrive(ref, index):
        pltpu.make_async_copy(ref, ref, recv_sem.at[index]).wait()

    def sent(ref, index, when=None):
        def wait():
            pltpu.make_async_copy(ref, ref, send_sem.at[index]).wait()
        waits.append((when, wait))

    def load(k):
        where = pl.ds(k * DEPTH, DEPTH)
        return pltpu.make_async_copy(design.at[:, where], raw.at[:, where], load_sem.at[k])

    fetch = pltpu.make_async_copy(targets, base, load_sem.at[STEPS])
    fetch.start()
    for k in range(STEPS):
        load(k).start()
    barrier = pltpu.get_barrier_semaphore()
    for to in plane + line + [twin]:
        pl.semaphore_signal(barrier, inc=1, device_id=to, device_id_type=MESH)

    def scaled(block, turn, groups):
        squares = jnp.broadcast_to(jnp.sum(block * block, axis=1, keepdims=True), (block.shape[0], 128))
        for i, g in enumerate(groups):
            x_row[turn, g, me] = as_row(squares[HALF * i:HALF * (i + 1)])
        norm = positive(jnp.sqrt(squares))
        norm = jnp.concatenate([norm, norm], axis=1)
        x_high, x_low = split(block / norm)
        return x_high, jnp.concatenate([x_high, x_low], axis=0)

    def product(x_high, both, k, turn, groups):
        rows = x_high.shape[0]
        where = pl.ds(k * DEPTH, DEPTH)
        first = jnp.dot(both, high[:, where], preferred_element_type=F32)
        second = jnp.dot(x_high, low[:, where], preferred_element_type=F32)
        result = first[:rows] + (first[rows:] + second)
        for i in range(2):
            h, j = divmod(2 * k + i, TILES)
            for n, g in enumerate(groups):
                partial[turn, pl.ds(8 * g + 4 * h, 4), j] = (
                    result[HALF * n:HALF * (n + 1), 128 * i:128 * (i + 1)].reshape(4, 8, 128)
                )

    places = ((y, x), (x, y))

    def chunk(g, way, place):
        return 8 * g + 4 * (place // 2) + 2 * way + lax.rem(place, 2)

    def around(way, leg):
        found = []
        for d in (2, 1, 3):
            if (way == 0) == (leg == 0):
                tx, ty = x, lax.rem(y + d, 4)
                found.append((ty, plane_id(tx, ty)))
            else:
                tx, ty = lax.rem(x + d, 4), y
                found.append((tx, plane_id(tx, ty)))
        return found

    def index_of(turn, g, way, step):
        return 32 + ((turn * 2 + g) * 2 + way) * 4 + step

    def scatter(turn, g):
        index = 2 * turn + g
        for to in plane:
            send(x_row.at[turn, g, me], x_row.at[turn, g, me], index, to)
        sent(x_row.at[turn, g, pl.ds(0, 15)], index)
        for way in range(2):
            index = index_of(turn, g, way, 0)
            for place, to in around(way, 0):
                send(
                    partial.at[turn, chunk(g, way, place), pl.ds(0, TILES)],
                    first_in.at[turn, g, way, places[way][0], pl.ds(0, TILES)], index, to,
                )
            sent(first_in.at[turn, g, way, pl.ds(0, 3), pl.ds(0, TILES)], index)

    def middle(turn, g):
        arrive(x_row.at[turn, g, pl.ds(0, 15)], 2 * turn + g)
        left_norms(turn, g)
        for way in range(2):
            here, there = places[way]
            eight = 2 * way + lax.rem(here, 2)
            norm = u_coef[turn, 4 * g + eight]

            def weight(place):
                row = 4 * x + place if way == 0 else 4 * place + y
                return jnp.sqrt(as_tile(x_row[turn, g, row], eight)) / norm

            total = partial[turn, chunk(g, way, here), pl.ds(0, TILES)] * weight(here)
            others = [(place, weight(place)) for place, _ in around(way, 0)]
            arrive(first_in.at[turn, g, way, pl.ds(0, 3), pl.ds(0, TILES)], index_of(turn, g, way, 0))
            for place, scale in others:
                total = total + first_in[turn, g, way, place, pl.ds(0, TILES)] * scale
            second_out[turn, g, way, pl.ds(0, TILES)] = total
            second_out[turn, g, way, TILES] = jnp.zeros((8, 128), F32)
            index = index_of(turn, g, way, 1)
            for place, to in around(way, 1):
                send(
                    second_out.at[turn, g, way, pl.ds(4 * place, 4)],
                    second_in.at[turn, g, way, there], index, to,
                )
            sent(second_in.at[turn, g, way, pl.ds(0, 3)], index)

    def spread(turn, g):
        for way in range(2):
            here, there = places[way]
            mine = pl.ds(4 * there, 4)
            which = chunk(g, way, here)
            eight = 4 * g + 2 * way + lax.rem(here, 2)
            total = second_out[turn, g, way, mine]
            if turn == 1:
                total = total - right[0, which, mine] * (u_coef[1, eight] / v_coef[0, eight])
            arrive(second_in.at[turn, g, way, pl.ds(0, 3)], index_of(turn, g, way, 1))
            for place, _ in around(way, 1):
                total = total + second_in[turn, g, way, place]
            right[turn, which, mine] = total
            index = index_of(turn, g, way, 2)
            for _, to in around(way, 1):
                send(right.at[turn, which, mine], right.at[turn, which, mine], index, to)
            sent(right.at[turn, 0, pl.ds(0, 12)], index)

    def widen(turn, g):
        for way in range(2):
            here, _ = places[way]
            which = chunk(g, way, here)
            arrive(right.at[turn, 0, pl.ds(0, 12)], index_of(turn, g, way, 2))
            index = index_of(turn, g, way, 3)
            for _, to in around(way, 0):
                send(right.at[turn, which, pl.ds(0, TILES)], right.at[turn, which, pl.ds(0, TILES)], index, to)
            sent(right.at[turn, pl.ds(0, 3), pl.ds(0, TILES)], index)

    def left_norms(turn, g):
        total = x_row[turn, g, 0]
        for s in range(1, 16):
            total = total + x_row[turn, g, s]
        u_coef[turn, pl.ds(4 * g, 4)] = jnp.sqrt(as_column(total))

    def forward(turn, g):
        for way in range(2):
            arrive(right.at[turn, pl.ds(0, 3), pl.ds(0, TILES)], index_of(turn, g, way, 3))
        slabs = [(pl.ds(8 * g + 4 * (j // TILES), 4), j % TILES) for j in range(2 * TILES)]
        squares = jnp.zeros((4, 8, 128), F32)
        for h, i in slabs:
            v = right[turn, h, i]
            squares = squares + v * v
        squares = lane_sum(squares)
        z_row[turn, g, z] = as_row(squares.reshape(HALF, 128))
        index = 12 + 2 * turn + g
        for to in line:
            send(z_row.at[turn, g, z], z_row.at[turn, g, z], index, to)
        sent(z_row.at[turn, g, pl.ds(0, 15)], index)
        inverse = 1.0 / positive(jnp.sqrt(squares))
        first = jnp.zeros((2 * HALF, DEPTH), F32)
        second = jnp.zeros((HALF, DEPTH), F32)
        contract = (((1,), (1,)), ((), ()))
        for k in range(STEPS):
            where = pl.ds(k * DEPTH, DEPTH)
            w = [(right[turn, h, i] * inverse).reshape(HALF, 128) for h, i in slabs[2 * k:2 * k + 2]]
            w_high, w_low = split(jnp.concatenate(w, axis=1))
            both = jnp.concatenate([w_high, w_low], axis=0)
            first = first + lax.dot_general(both, high[:, where], contract, preferred_element_type=F32)
            second = second + lax.dot_general(w_high, low[:, where], contract, preferred_element_type=F32)
        result = first[:HALF] + (first[HALF:] + second)
        for n in range(2):
            line_out[turn, pl.ds(8 * g + 4 * n, 4)] = result[:, 128 * n:128 * (n + 1)].reshape(4, 8, 128)
        index = 16 + 2 * turn + g
        swap = lax.rem(z_parity + g, 2)
        for i in range(8):
            even, odd = LINE_EVEN[i], LINE_ODD[i]
            tz = lax.rem(z + even + (odd - even) * swap, 16)

            def push():
                send(
                    line_out.at[turn, 8 * g + tz // 2], line_in.at[turn, z], index,
                    {"row": me, "col": 2 * tz + core},
                )

            if i < 7:
                push()
            else:
                pl.when(swap == 1)(push)
        sent(line_in.at[turn, pl.ds(0, 7)], index, swap == 0)
        sent(line_in.at[turn, pl.ds(0, 8)], index, swap == 1)

        @pl.when(swap == 0)
        def _():
            line_in[turn, z] = line_out[turn, my_tile]

    def tile_sum(turn, g):
        mine = z_parity == g
        arrive(z_row.at[turn, g, pl.ds(0, 15)], 12 + 2 * turn + g)
        total = z_row[turn, g, 0]
        for s in range(1, 16):
            total = total + z_row[turn, g, s]
        twin_out[turn, g] = total
        index = 20 + 2 * turn + g
        send(twin_out.at[turn, g], twin_in.at[turn, g], index, twin)
        sent(twin_out.at[turn, g], index)

        @pl.when(mine)
        def _():
            weights = [jnp.sqrt(as_tile(z_row[turn, g, s], tile_group)) for s in range(16)]
            norm = positive(jnp.sqrt(as_tile(twin_out[turn, g], tile_group)))
            arrive(line_in.at[turn, pl.ds(0, 15)], 16 + 2 * turn + g)
            part = line_in[turn, 0] * (weights[0] / norm)
            for s in range(1, 16):
                part = part + line_in[turn, s] * (weights[s] / norm)
            tile_out[turn] = part
            send(tile_out.at[turn], tile_in.at[turn], 24 + turn, twin)
        sent(tile_out.at[turn], 24 + turn, mine)
        arrive(twin_in.at[turn, g], index)
        v_coef[turn, pl.ds(4 * g, 4)] = jnp.sqrt(as_column(twin_out[turn, g] + twin_in[turn, g]))

        @pl.when(mine)
        def _():
            own = jnp.sqrt(as_tile(twin_out[turn, g], tile_group))
            other = jnp.sqrt(as_tile(twin_in[turn, g], tile_group))
            v_norm = v_coef[turn, 4 * g + tile_group]
            if turn == 0:
                half = pl.ds(128 * (z // 8), 128)
                where = pl.ds(pl.multiple_of(HALF * g + 8 * tile_group, 8), 8)
                before = base[where, half]
            else:
                before = left[my_tile]
            unit = before / u_coef[turn, 4 * g + tile_group]
            arrive(tile_in.at[turn], 24 + turn)
            tile = tile_out[turn] * (own / v_norm) + tile_in[turn] * (other / v_norm) - v_norm * unit
            if turn == 0:
                left[my_tile] = tile
                for to in line:
                    send(left.at[my_tile], left.at[my_tile], 26 + g, to)
            else:
                end_xy[me] = lane_sum(tile * tile)
                for to in plane:
                    send(end_xy.at[me], end_xy.at[me], 28, to)
        if turn == 0:
            sent(left.at[pl.ds(0, 15)], 26 + g, mine)
        else:
            sent(end_xy.at[pl.ds(0, 15)], 28, mine)

    def back(g):
        pl.when(z_parity == g)(lambda: arrive(left.at[pl.ds(0, 7)], 26 + g))
        pl.when(z_parity != g)(lambda: arrive(left.at[pl.ds(0, 8)], 26 + g))
        block = [left[pl.ds(8 * g + 4 * n, 4)].reshape(HALF, 128) for n in range(2)]
        x_high, both = scaled(jnp.concatenate(block, axis=1), 1, [g])
        for k in range(STEPS):
            product(x_high, both, k, 1, [g])
        scatter(1, g)

    def tile_end(g):
        mine = z_parity == g

        @pl.when(mine)
        def _():
            arrive(end_xy.at[pl.ds(0, 15)], 28)
            total = end_xy[0]
            for s in range(1, 16):
                total = total + end_xy[s]
            end_z[my_tile] = total
            for to in line:
                send(end_z.at[my_tile], end_z.at[my_tile], 29 + g, to)
        sent(end_z.at[pl.ds(0, 15)], 29 + g, mine)

    def combine(g):
        pl.when(z_parity == g)(lambda: arrive(end_z.at[pl.ds(0, 7)], 29 + g))
        pl.when(z_parity != g)(lambda: arrive(end_z.at[pl.ds(0, 8)], 29 + g))
        where = pl.ds(4 * g, 4)
        phi_bar, u_first = u_coef[0, where], u_coef[1, where]
        v_first, v_second = v_coef[0, where], v_coef[1, where]
        u_second = jnp.sqrt(end_z[pl.ds(8 * g, 4)] + end_z[pl.ds(8 * g + 4, 4)])
        rho = jnp.sqrt(v_first * v_first + u_first * u_first)
        cosine, sine = v_first / rho, u_first / rho
        step = cosine * phi_bar / rho
        phi_bar = sine * phi_bar
        rho_bar = -cosine * v_second
        turn_back = sine * v_second / rho
        rho = jnp.sqrt(rho_bar * rho_bar + u_second * u_second)
        step_second = (rho_bar / rho) * phi_bar / rho
        for_first = (step - step_second * turn_back) / v_first
        for_second = step_second / v_second
        for j in range(2 * TILES):
            h, i = pl.ds(8 * g + 4 * (j // TILES), 4), j % TILES
            value = right[0, h, i] * for_first + right[1, h, i] * for_second
            out[pl.ds(HALF * g, HALF), pl.ds(128 * j, 128)] = value.reshape(HALF, 128)

    fetch.wait()
    x_high, both = scaled(base[...], 0, [0, 1])
    for k in range(STEPS):
        load(k).wait()
        where = pl.ds(k * DEPTH, DEPTH)
        d_high, d_low = split(raw[:, where])
        high[:, where] = d_high
        low[:, where] = d_low
        product(x_high, both, k, 0, [0, 1])
    pl.semaphore_wait(barrier, 31)
    for g in range(2):
        scatter(0, g)
    for step in (middle, spread, widen):
        for g in range(2):
            step(0, g)
    forward(0, 0)
    forward(0, 1)
    tile_sum(0, 0)
    tile_sum(0, 1)
    back(0)
    back(1)
    for step in (middle, spread, widen):
        for g in range(2):
            step(1, g)
    forward(1, 0)
    forward(1, 1)
    tile_sum(1, 0)
    tile_sum(1, 1)
    tile_end(0)
    tile_end(1)
    combine(0)
    combine(1)
    for when, wait in waits:
        if when is None:
            wait()
        else:
            pl.when(when)(wait)


def local(design, targets):
    tile = (8, 128)
    return pl.pallas_call(
        kernel,
        out_shape=jax.ShapeDtypeStruct((SETS, COLS), F32),
        in_specs=[pl.BlockSpec(memory_space=pltpu.HBM)] * 2,
        out_specs=pl.BlockSpec(memory_space=pltpu.VMEM),
        scratch_shapes=[
            pltpu.VMEM((DEPTH, COLS), F32),
            pltpu.VMEM((DEPTH, COLS), BF16),
            pltpu.VMEM((DEPTH, COLS), BF16),
            pltpu.VMEM((SETS, DEPTH), F32),
            pltpu.VMEM((2, 16, 16) + tile, F32),
            pltpu.VMEM((2, 2, 2, 4, 16) + tile, F32),
            pltpu.VMEM((2, 2, 2, 16) + tile, F32),
            pltpu.VMEM((2, 2, 2, 4, 4) + tile, F32),
            pltpu.VMEM((2, 16, 16) + tile, F32),
            pltpu.VMEM((2, 2, 16, 1, 128), F32),
            pltpu.VMEM((2, 2, 16, 1, 128), F32),
            pltpu.VMEM((2, 2, 1, 128), F32),
            pltpu.VMEM((2, 2, 1, 128), F32),
            pltpu.VMEM((2, 16) + tile, F32),
            pltpu.VMEM((2, 16) + tile, F32),
            pltpu.VMEM((2,) + tile, F32),
            pltpu.VMEM((2,) + tile, F32),
            pltpu.VMEM((16,) + tile, F32),
            pltpu.VMEM((2, 8) + tile, F32),
            pltpu.VMEM((2, 8) + tile, F32),
            pltpu.VMEM((16,) + tile, F32),
            pltpu.VMEM((16,) + tile, F32),
            pltpu.SemaphoreType.DMA((STEPS + 1,)),
            pltpu.SemaphoreType.DMA((64,)),
            pltpu.SemaphoreType.DMA((64,)),
        ],
        compiler_params=pltpu.CompilerParams(
            collective_id=0, has_side_effects=True, vmem_limit_bytes=61 << 20
        ),
    )(design, targets)


def solution(mesh):
    in_specs = (P("row", "col"), P(None, "row"))
    return jax.shard_map(local, mesh=mesh, in_specs=in_specs, out_specs=P(None, "col"), check_vma=False)
```

```python
import jax
import jax.numpy as jnp
from jax import lax
from jax.experimental import pallas as pl
from jax.experimental.pallas import tpu as pltpu
from jax.sharding import PartitionSpec as P

MESH = pl.DeviceIdType.MESH
F32 = jnp.float32
BF16 = jnp.bfloat16
SETS = 64
HALF = 32
DEPTH = 256
COLS = 3840
TILES = 15
STEPS = COLS // DEPTH
FAR_FIRST = [(2, 2), (2, 1), (2, 3), (1, 2), (3, 2), (2, 0), (0, 2), (1, 1), (3, 3), (1, 3), (3, 1), (0, 1), (0, 3), (1, 0), (3, 0)]


def split(x):
    high = x.astype(BF16)
    low = (x - high.astype(F32)).astype(BF16)
    return high, low


def lane_sum(x):
    return jnp.broadcast_to(jnp.sum(x, axis=-1, keepdims=True), x.shape)


def as_row(column):
    at = lax.broadcasted_iota(jnp.int32, (HALF, 128), 0) == lax.broadcasted_iota(jnp.int32, (HALF, 128), 1)
    return jnp.sum(jnp.where(at, column, 0.0), axis=0, keepdims=True)


def as_column(row):
    at = lax.broadcasted_iota(jnp.int32, (HALF, 128), 0) == lax.broadcasted_iota(jnp.int32, (HALF, 128), 1)
    return lane_sum(jnp.where(at, jnp.broadcast_to(row, (HALF, 128)), 0.0)).reshape(4, 8, 128)


def as_tile(row, group):
    sets = lax.broadcasted_iota(jnp.int32, (8, 128), 0) + 8 * group
    at = sets == lax.broadcasted_iota(jnp.int32, (8, 128), 1)
    return lane_sum(jnp.where(at, jnp.broadcast_to(row, (8, 128)), 0.0))


def tile_row(tile, group):
    sets = lax.broadcasted_iota(jnp.int32, (8, 128), 0) + 8 * group
    at = sets == lax.broadcasted_iota(jnp.int32, (8, 128), 1)
    return jnp.sum(jnp.where(at, tile, 0.0), axis=0, keepdims=True)


def positive(x):
    return jnp.where(x > 0.0, x, 1.0)


def kernel(
    design, targets, out,
    raw, high, low, high_turned, low_turned, base, partial, first_in, second_in, right, z_row, twin_out, twin_in, line_out, line_in,
    halves, half_in, left, v_coef, u_coef, end_xy, end_z,
    load_sem, send_sem, recv_sem, greeting,
):
    me = lax.axis_index("row")
    col = lax.axis_index("col")
    x, y = me // 4, lax.rem(me, 4)
    z, core = col // 2, lax.rem(col, 2)
    firsts = ((8, 9), (12, 13))

    def owner(turn, g, k):
        return lax.rem(firsts[turn][g] + 2 * k, 16)

    def owned(turn, g):
        ahead = lax.rem(z + 16 - firsts[turn][g], 16)
        return (ahead < 8) & (lax.rem(ahead, 2) == 0), lax.rem(ahead // 2, 4)

    def in_plane(dx, dy):
        return lax.rem(x + dx, 4), lax.rem(y + dy, 4)

    def plane_id(tx, ty):
        return {"row": tx * 4 + ty, "col": col}

    plane = [plane_id(*in_plane(*d)) for d in FAR_FIRST]
    line = [
        {"row": me, "col": lax.rem(col + 2 * d, 32)}
        for d in (8, 7, 9, 6, 10, 5, 11, 4, 12, 3, 13, 2, 14, 1, 15)
    ]
    twin = {"row": me, "col": 2 * z + 1 - core}
    other_line = [{"row": me, "col": lax.rem(2 * (z + d) + 1 - core, 32)} for d in range(1, 16)]
    on_line = {d: {"row": me, "col": lax.rem(col + 2 * d, 32)} for d in (1, 2, 4, 12, 14, 15)}
    near = [plane_id(*in_plane(d, 0)) for d in (1, 2, 3)] + [plane_id(*in_plane(0, d)) for d in (1, 2, 3)]
    near = near + [on_line[d] for d in (1, 2, 14, 15)] + [twin]

    def greet(n, distance):
        for d in (distance, 16 - distance):
            pl.semaphore_signal(greeting.at[n], inc=1, device_id=on_line[d], device_id_type=MESH)

    def greeted(n):
        pl.semaphore_wait(greeting.at[n], 2)

    waits = []

    def send(src, dst, index, to):
        pltpu.make_async_remote_copy(
            src_ref=src, dst_ref=dst, send_sem=send_sem.at[index], recv_sem=recv_sem.at[index],
            device_id=to, device_id_type=MESH,
        ).start()

    def arrive(ref, index):
        pltpu.make_async_copy(ref, ref, recv_sem.at[index]).wait()

    def sent(ref, index, when=None):
        def wait():
            pltpu.make_async_copy(ref, ref, send_sem.at[index]).wait()
        waits.append((when, wait))

    def load(k):
        where = pl.ds(k * DEPTH, DEPTH)
        return pltpu.make_async_copy(design.at[:, where], raw.at[:, where], load_sem.at[k])

    fetch = pltpu.make_async_copy(targets, base, load_sem.at[STEPS])
    fetch.start()
    for k in range(STEPS):
        load(k).start()
    barrier = pltpu.get_barrier_semaphore()
    for to in near:
        pl.semaphore_signal(barrier, inc=1, device_id=to, device_id_type=MESH)

    def scaled(block, turn, groups):
        squares = jnp.broadcast_to(jnp.sum(block * block, axis=1, keepdims=True), (block.shape[0], 128))
        for i, g in enumerate(groups):
            for h in range(2):
                partial[turn, pl.ds(8 * g + 4 * h, 4), TILES] = squares[HALF * i:HALF * (i + 1)].reshape(4, 8, 128)
        norm = positive(jnp.sqrt(squares))
        norm = jnp.concatenate([norm, norm], axis=1)
        x_high, x_low = split(block / norm)
        return x_high, jnp.concatenate([x_high, x_low], axis=0)

    def product(x_high, both, k, turn, groups):
        rows = x_high.shape[0]
        where = pl.ds(k * DEPTH, DEPTH)
        first = jnp.dot(both, high[:, where], preferred_element_type=F32)
        second = jnp.dot(x_high, low[:, where], preferred_element_type=F32)
        result = first[:rows] + (first[rows:] + second)
        for i in range(2):
            h, j = divmod(2 * k + i, TILES)
            for n, g in enumerate(groups):
                partial[turn, pl.ds(8 * g + 4 * h, 4), j] = (
                    result[HALF * n:HALF * (n + 1), 128 * i:128 * (i + 1)].reshape(4, 8, 128)
                )

    places = ((y, x), (x, y))

    def chunk(g, way, place):
        return 8 * g + 4 * (place // 2) + 2 * way + lax.rem(place, 2)

    def around(way, leg):
        found = []
        for d in (2, 1, 3):
            if (way == 0) == (leg == 0):
                tx, ty = x, lax.rem(y + d, 4)
                found.append((ty, plane_id(tx, ty)))
            else:
                tx, ty = lax.rem(x + d, 4), y
                found.append((tx, plane_id(tx, ty)))
        return found

    def index_of(turn, g, way, step):
        return 64 + ((turn * 2 + g) * 2 + way) * 3 + step

    def scatter(turn, g):
        for way in range(2):
            index = index_of(turn, g, way, 0)
            for place, to in around(way, 0):
                send(
                    partial.at[turn, chunk(g, way, place)], first_in.at[turn, g, way, places[way][0]], index, to
                )
            sent(first_in.at[turn, g, way, pl.ds(0, 3)], index)

    def summed(parts):
        squares = [part[TILES] for part in parts]
        square = (squares[0] + squares[1]) + (squares[2] + squares[3])
        norm = jnp.sqrt(square)
        inverse = 1.0 / positive(norm)
        total = jnp.zeros((TILES, 8, 128), F32)
        for part, w in zip(parts, squares):
            total = total + part[pl.ds(0, TILES)] * (jnp.sqrt(w) * inverse)
        return total, square, norm

    def middle(turn, g):
        for way in range(2):
            here, there = places[way]
            which = chunk(g, way, here)
            arrive(first_in.at[turn, g, way, pl.ds(0, 3)], index_of(turn, g, way, 0))
            parts = [partial.at[turn, which]] + [first_in.at[turn, g, way, place] for place, _ in around(way, 0)]
            total, square, _ = summed(parts)
            second_in[turn, g, way, there, pl.ds(0, TILES)] = total
            second_in[turn, g, way, there, TILES] = square
            index = index_of(turn, g, way, 1)
            for _, to in around(way, 1):
                send(second_in.at[turn, g, way, there], second_in.at[turn, g, way, there], index, to)
            sent(second_in.at[turn, g, way, pl.ds(0, 3)], index)

    def spread(turn, g):
        for way in range(2):
            here, _ = places[way]
            which = chunk(g, way, here)
            arrive(second_in.at[turn, g, way, pl.ds(0, 3)], index_of(turn, g, way, 1))
            total, square, norm = summed([second_in.at[turn, g, way, place] for place in range(4)])
            if turn == 1:
                v_norm = v_coef[0, 4 * g + 2 * way + lax.rem(here, 2)]
                total = total - right[0, which, pl.ds(0, TILES)] * (norm / v_norm)
            right[turn, which, pl.ds(0, TILES)] = total
            right[turn, which, TILES] = square
            index = index_of(turn, g, way, 2)
            for _, to in around(way, 0):
                send(right.at[turn, which], right.at[turn, which], index, to)
            sent(right.at[turn, pl.ds(0, 3)], index)

    def forward(turn, g):
        for way in range(2):
            arrive(right.at[turn, pl.ds(0, 3)], index_of(turn, g, way, 2))
        u_coef[turn, pl.ds(4 * g, 4)] = jnp.sqrt(right[turn, pl.ds(8 * g, 4), TILES])
        slabs = [(pl.ds(8 * g + 4 * (j // TILES), 4), j % TILES) for j in range(2 * TILES)]
        squares = jnp.zeros((4, 8, 128), F32)
        for h, i in slabs:
            v = right[turn, h, i]
            squares = squares + v * v
        squares = lane_sum(squares)
        twin_out[turn, g] = as_row(squares.reshape(HALF, 128))
        send(twin_out.at[turn, g], twin_in.at[turn, g], 20 + 2 * turn + g, twin)
        sent(twin_out.at[turn, g], 20 + 2 * turn + g)
        inverse = 1.0 / positive(jnp.sqrt(squares))
        first = jnp.zeros((2 * HALF, DEPTH), F32)
        second = jnp.zeros((HALF, DEPTH), F32)
        for k in range(STEPS):
            where = pl.ds(k * DEPTH, DEPTH)
            w = [(right[turn, h, i] * inverse).reshape(HALF, 128) for h, i in slabs[2 * k:2 * k + 2]]
            w_high, w_low = split(jnp.concatenate(w, axis=1))
            both = jnp.concatenate([w_high, w_low], axis=0)
            first = first + jnp.dot(both, high_turned[where, :], preferred_element_type=F32)
            second = second + jnp.dot(w_high, low_turned[where, :], preferred_element_type=F32)
        result = first[:HALF] + (first[HALF:] + second)
        for n in range(2):
            halves[turn, g, n] = result[:, 128 * n:128 * (n + 1)].reshape(4, 8, 128)
        index = 24 + 2 * turn + g
        send(halves.at[turn, g, 1 - core], half_in.at[turn, g], index, twin)
        sent(half_in.at[turn, g], index)
        arrive(twin_in.at[turn, g], 20 + 2 * turn + g)
        z_row[turn, g, z] = twin_out[turn, g] + twin_in[turn, g]
        other = as_column(twin_in[turn, g])
        inverse = 1.0 / positive(jnp.sqrt(squares + other))
        own, other = jnp.sqrt(squares) * inverse, jnp.sqrt(other) * inverse
        for to in line:
            send(z_row.at[turn, g, z], z_row.at[turn, g, z], 12 + 2 * turn + g, to)
        sent(z_row.at[turn, g, pl.ds(0, 15)], 12 + 2 * turn + g)
        arrive(half_in.at[turn, g], index)
        line_out[turn, g] = halves[turn, g, core] * own + half_in[turn, g] * other
        index = 16 + 2 * turn + g
        mine, my_eight = owned(turn, g)
        for k in range(4):
            to = owner(turn, g, k)

            @pl.when(to != z)
            def _():
                send(line_out.at[turn, g, k], line_in.at[turn, g, z], index, {"row": me, "col": 2 * to + core})

        @pl.when(mine)
        def _():
            line_in[turn, g, z] = line_out[turn, g, my_eight]

        sent(line_in.at[turn, g, pl.ds(0, 3)], index, mine)
        sent(line_in.at[turn, g, pl.ds(0, 4)], index, jnp.logical_not(mine))

    def tile_sum(turn, g):
        mine, eight = owned(turn, g)
        arrive(z_row.at[turn, g, pl.ds(0, 15)], 12 + 2 * turn + g)
        total = z_row[turn, g, 0]
        for s in range(1, 16):
            total = total + z_row[turn, g, s]
        v_coef[turn, pl.ds(4 * g, 4)] = jnp.sqrt(as_column(total))

        @pl.when(mine)
        def _():
            v_norm = v_coef[turn, 4 * g + eight]
            inverse = 1.0 / v_norm
            weights = [jnp.sqrt(as_tile(z_row[turn, g, s], eight)) * inverse for s in range(16)]
            if turn == 0:
                where = pl.ds(pl.multiple_of(HALF * g + 8 * eight, 8), 8)
                before = base[where, pl.ds(pl.multiple_of(128 * core, 128), 128)]
            else:
                before = left[g, core, eight]
            before = before * (v_norm / u_coef[turn, 4 * g + eight])
            arrive(line_in.at[turn, g, pl.ds(0, 15)], 16 + 2 * turn + g)
            tile = line_in[turn, g, 0] * weights[0]
            for s in range(1, 16):
                tile = tile + line_in[turn, g, s] * weights[s]
            tile = tile - before
            if turn == 0:
                left[g, core, eight] = tile
                for to in line:
                    send(left.at[g, core, eight], left.at[g, core, eight], 28 + g, to)
            else:
                end_xy[g, me] = tile_row(lane_sum(tile * tile), eight)
                for to in plane:
                    send(end_xy.at[g, me], end_xy.at[g, me], 60 + g, to)
        if turn == 0:
            sent(line_in.at[0, g, pl.ds(0, 15)], 28 + g, mine)
        else:
            sent(end_xy.at[g, pl.ds(0, 15)], 60 + g, mine)

    def back(g):
        mine, _ = owned(0, g)
        pl.when(mine)(lambda: arrive(left.at[g, 0, pl.ds(0, 3)], 28 + g))
        pl.when(jnp.logical_not(mine))(lambda: arrive(left.at[g, 0], 28 + g))
        send(left.at[g, core], left.at[g, core], 30 + g, twin)
        sent(left.at[g, 0], 30 + g)
        arrive(left.at[g, 0], 30 + g)
        block = [left[g, n].reshape(HALF, 128) for n in range(2)]
        x_high, both = scaled(jnp.concatenate(block, axis=1), 1, [g])
        for k in range(STEPS):
            product(x_high, both, k, 1, [g])
        scatter(1, g)

    def tile_end(g):
        mine, eight = owned(1, g)

        @pl.when(mine)
        def _():
            arrive(end_xy.at[g, pl.ds(0, 15)], 60 + g)
            total = end_xy[g, 0]
            for s in range(1, 16):
                total = total + end_xy[g, s]
            end_z[g, core, eight] = total
            for to in line:
                send(end_z.at[g, core, eight], end_z.at[g, core, eight], 62 + g, to)
            for to in other_line + [twin]:
                send(end_z.at[g, core, eight], end_z.at[g, core, eight], 32 + g, to)
        sent(end_xy.at[g, pl.ds(0, 15)], 62 + g, mine)
        sent(end_xy.at[g], 32 + g, mine)

    def combine(g):
        mine, _ = owned(1, g)
        pl.when(mine)(lambda: arrive(end_z.at[g, 0, pl.ds(0, 3)], 62 + g))
        pl.when(jnp.logical_not(mine))(lambda: arrive(end_z.at[g, 0], 62 + g))
        arrive(end_z.at[g, 0], 32 + g)
        where = pl.ds(4 * g, 4)
        phi_bar, u_first = u_coef[0, where], u_coef[1, where]
        v_first, v_second = v_coef[0, where], v_coef[1, where]
        ends = [end_z[g, n, k] for n in range(2) for k in range(4)]
        total = ends[0]
        for end in ends[1:]:
            total = total + end
        u_second = jnp.sqrt(as_column(total))
        rho = jnp.sqrt(v_first * v_first + u_first * u_first)
        cosine, sine = v_first / rho, u_first / rho
        step = cosine * phi_bar / rho
        phi_bar = sine * phi_bar
        rho_bar = -cosine * v_second
        turn_back = sine * v_second / rho
        rho = jnp.sqrt(rho_bar * rho_bar + u_second * u_second)
        step_second = (rho_bar / rho) * phi_bar / rho
        for_first = (step - step_second * turn_back) / v_first
        for_second = step_second / v_second
        for j in range(2 * TILES):
            h, i = pl.ds(8 * g + 4 * (j // TILES), 4), j % TILES
            value = right[0, h, i] * for_first + right[1, h, i] * for_second
            out[pl.ds(HALF * g, HALF), pl.ds(128 * j, 128)] = value.reshape(HALF, 128)

    def turn_over(start, stop):
        for k in range(start, stop):
            where = pl.ds(k * DEPTH, DEPTH)
            d_high, d_low = split(jnp.transpose(raw[:, where]))
            high_turned[where, :] = d_high
            low_turned[where, :] = d_low

    fetch.wait()
    x_high, both = scaled(base[...], 0, [0, 1])
    for k in range(STEPS):
        load(k).wait()
        where = pl.ds(k * DEPTH, DEPTH)
        d_high, d_low = split(raw[:, where])
        high[:, where] = d_high
        low[:, where] = d_low
        product(x_high, both, k, 0, [0, 1])
    pl.semaphore_wait(barrier, 11)
    for g in range(2):
        scatter(0, g)
    greet(0, 2)
    turn_over(0, 5)
    for g in range(2):
        middle(0, g)
    greeted(0)
    greet(1, 4)
    turn_over(5, 10)
    for g in range(2):
        spread(0, g)
    turn_over(10, STEPS)
    greeted(1)
    forward(0, 0)
    forward(0, 1)
    tile_sum(0, 0)
    tile_sum(0, 1)
    back(0)
    back(1)
    for step in (middle, spread):
        for g in range(2):
            step(1, g)
    forward(1, 0)
    forward(1, 1)
    tile_sum(1, 0)
    tile_sum(1, 1)
    tile_end(0)
    tile_end(1)
    combine(0)
    combine(1)
    for when, wait in waits:
        if when is None:
            wait()
        else:
            pl.when(when)(wait)


def local(design, targets):
    tile = (8, 128)
    return pl.pallas_call(
        kernel,
        out_shape=jax.ShapeDtypeStruct((SETS, COLS), F32),
        in_specs=[pl.BlockSpec(memory_space=pltpu.HBM)] * 2,
        out_specs=pl.BlockSpec(memory_space=pltpu.VMEM),
        scratch_shapes=[
            pltpu.VMEM((DEPTH, COLS), F32),
            pltpu.VMEM((DEPTH, COLS), BF16),
            pltpu.VMEM((DEPTH, COLS), BF16),
            pltpu.VMEM((COLS, DEPTH), BF16),
            pltpu.VMEM((COLS, DEPTH), BF16),
            pltpu.VMEM((SETS, DEPTH), F32),
            pltpu.VMEM((2, 16, 16) + tile, F32),
            pltpu.VMEM((2, 2, 2, 4, 16) + tile, F32),
            pltpu.VMEM((2, 2, 2, 4, 16) + tile, F32),
            pltpu.VMEM((2, 16, 16) + tile, F32),
            pltpu.VMEM((2, 2, 16, 1, 128), F32),
            pltpu.VMEM((2, 2, 1, 128), F32),
            pltpu.VMEM((2, 2, 1, 128), F32),
            pltpu.VMEM((2, 2, 4) + tile, F32),
            pltpu.VMEM((2, 2, 16) + tile, F32),
            pltpu.VMEM((2, 2, 2, 4) + tile, F32),
            pltpu.VMEM((2, 2, 4) + tile, F32),
            pltpu.VMEM((2, 2, 4) + tile, F32),
            pltpu.VMEM((2, 8) + tile, F32),
            pltpu.VMEM((2, 8) + tile, F32),
            pltpu.VMEM((2, 16, 1, 128), F32),
            pltpu.VMEM((2, 2, 4, 1, 128), F32),
            pltpu.SemaphoreType.DMA((STEPS + 1,)),
            pltpu.SemaphoreType.DMA((88,)),
            pltpu.SemaphoreType.DMA((88,)),
            pltpu.SemaphoreType.REGULAR((2,)),
        ],
        compiler_params=pltpu.CompilerParams(
            collective_id=0, has_side_effects=True, vmem_limit_bytes=61 << 20
        ),
    )(design, targets)


def solution(mesh):
    in_specs = (P("row", "col"), P(None, "row"))
    return jax.shard_map(local, mesh=mesh, in_specs=in_specs, out_specs=P(None, "col"), check_vma=False)
```

```python
import jax
import jax.numpy as jnp
from jax import lax
from jax.experimental import pallas as pl
from jax.experimental.pallas import tpu as pltpu
from jax.sharding import PartitionSpec as P

MESH = pl.DeviceIdType.MESH
F32 = jnp.float32
BF16 = jnp.bfloat16
SETS = 64
HALF = 32
DEPTH = 256
COLS = 3840
TILES = 15
STEPS = COLS // DEPTH
FAR_FIRST = [(2, 2), (2, 1), (2, 3), (1, 2), (3, 2), (2, 0), (0, 2), (1, 1), (3, 3), (1, 3), (3, 1), (0, 1), (0, 3), (1, 0), (3, 0)]


def split(x):
    high = x.astype(BF16)
    low = (x - high.astype(F32)).astype(BF16)
    return high, low


def lane_sum(x):
    return jnp.broadcast_to(jnp.sum(x, axis=-1, keepdims=True), x.shape)


def as_row(column):
    at = lax.broadcasted_iota(jnp.int32, (HALF, 128), 0) == lax.broadcasted_iota(jnp.int32, (HALF, 128), 1)
    return jnp.sum(jnp.where(at, column, 0.0), axis=0, keepdims=True)


def as_column(row):
    at = lax.broadcasted_iota(jnp.int32, (HALF, 128), 0) == lax.broadcasted_iota(jnp.int32, (HALF, 128), 1)
    return lane_sum(jnp.where(at, jnp.broadcast_to(row, (HALF, 128)), 0.0)).reshape(4, 8, 128)


def as_tile(row, group):
    sets = lax.broadcasted_iota(jnp.int32, (8, 128), 0) + 8 * group
    at = sets == lax.broadcasted_iota(jnp.int32, (8, 128), 1)
    return lane_sum(jnp.where(at, jnp.broadcast_to(row, (8, 128)), 0.0))


def tile_row(tile, group):
    sets = lax.broadcasted_iota(jnp.int32, (8, 128), 0) + 8 * group
    at = sets == lax.broadcasted_iota(jnp.int32, (8, 128), 1)
    return jnp.sum(jnp.where(at, tile, 0.0), axis=0, keepdims=True)


def positive(x):
    return jnp.where(x > 0.0, x, 1.0)


def kernel(
    design, targets, out,
    raw, high, low, high_turned, low_turned, base, partial, first_in, second_in, right, z_row, twin_out, twin_in, line_out, line_in,
    halves, half_in, left, v_coef, u_coef, end_xy, end_z,
    load_sem, send_sem, recv_sem, greeting,
):
    me = lax.axis_index("row")
    col = lax.axis_index("col")
    x, y = me // 4, lax.rem(me, 4)
    z, core = col // 2, lax.rem(col, 2)
    firsts = ((4, 5), (12, 13))

    def owner(turn, g, k):
        return lax.rem(firsts[turn][g] + 2 * k, 16)

    def owned(turn, g):
        ahead = lax.rem(z + 16 - firsts[turn][g], 16)
        return (ahead < 8) & (lax.rem(ahead, 2) == 0), lax.rem(ahead // 2, 4)

    def in_plane(dx, dy):
        return lax.rem(x + dx, 4), lax.rem(y + dy, 4)

    def plane_id(tx, ty):
        return {"row": tx * 4 + ty, "col": col}

    plane = [plane_id(*in_plane(*d)) for d in FAR_FIRST]
    line = [
        {"row": me, "col": lax.rem(col + 2 * d, 32)}
        for d in (8, 7, 9, 6, 10, 5, 11, 4, 12, 3, 13, 2, 14, 1, 15)
    ]
    twin = {"row": me, "col": 2 * z + 1 - core}
    other_line = [{"row": me, "col": lax.rem(2 * (z + d) + 1 - core, 32)} for d in range(1, 16)]
    on_line = {d: {"row": me, "col": lax.rem(col + 2 * d, 32)} for d in (1, 2, 4, 12, 14, 15)}
    near = [plane_id(*in_plane(d, 0)) for d in (1, 2, 3)] + [plane_id(*in_plane(0, d)) for d in (1, 2, 3)]
    near = near + [on_line[d] for d in (1, 2, 14, 15)] + [twin]

    def greet(n, distance):
        for d in (distance, 16 - distance):
            pl.semaphore_signal(greeting.at[n], inc=1, device_id=on_line[d], device_id_type=MESH)

    def greeted(n):
        pl.semaphore_wait(greeting.at[n], 2)

    waits = []

    def send(src, dst, index, to):
        pltpu.make_async_remote_copy(
            src_ref=src, dst_ref=dst, send_sem=send_sem.at[index], recv_sem=recv_sem.at[index],
            device_id=to, device_id_type=MESH,
        ).start()

    def arrive(ref, index):
        pltpu.make_async_copy(ref, ref, recv_sem.at[index]).wait()

    def sent(ref, index, when=None):
        def wait():
            pltpu.make_async_copy(ref, ref, send_sem.at[index]).wait()
        waits.append((when, wait))

    def load(k):
        where = pl.ds(k * DEPTH, DEPTH)
        return pltpu.make_async_copy(design.at[:, where], raw.at[:, where], load_sem.at[k])

    fetch = pltpu.make_async_copy(targets, base, load_sem.at[STEPS])
    fetch.start()
    for k in range(STEPS):
        load(k).start()
    barrier = pltpu.get_barrier_semaphore()
    for to in near:
        pl.semaphore_signal(barrier, inc=1, device_id=to, device_id_type=MESH)

    def scaled(block, turn, groups):
        squares = jnp.broadcast_to(jnp.sum(block * block, axis=1, keepdims=True), (block.shape[0], 128))
        for i, g in enumerate(groups):
            for h in range(2):
                partial[turn, pl.ds(8 * g + 4 * h, 4), TILES] = squares[HALF * i:HALF * (i + 1)].reshape(4, 8, 128)
        norm = positive(jnp.sqrt(squares))
        norm = jnp.concatenate([norm, norm], axis=1)
        x_high, x_low = split(block / norm)
        return x_high, jnp.concatenate([x_high, x_low], axis=0)

    def product(x_high, both, k, turn, groups):
        rows = x_high.shape[0]
        where = pl.ds(k * DEPTH, DEPTH)
        first = jnp.dot(both, high[:, where], preferred_element_type=F32)
        second = jnp.dot(x_high, low[:, where], preferred_element_type=F32)
        result = first[:rows] + (first[rows:] + second)
        for i in range(2):
            h, j = divmod(2 * k + i, TILES)
            for n, g in enumerate(groups):
                partial[turn, pl.ds(8 * g + 4 * h, 4), j] = (
                    result[HALF * n:HALF * (n + 1), 128 * i:128 * (i + 1)].reshape(4, 8, 128)
                )

    places = ((y, x), (x, y))

    def chunk(g, way, place):
        return 8 * g + 4 * (place // 2) + 2 * way + lax.rem(place, 2)

    def around(way, leg):
        found = []
        for d in (2, 1, 3):
            if (way == 0) == (leg == 0):
                tx, ty = x, lax.rem(y + d, 4)
                found.append((ty, plane_id(tx, ty)))
            else:
                tx, ty = lax.rem(x + d, 4), y
                found.append((tx, plane_id(tx, ty)))
        return found

    def index_of(turn, g, way, step):
        return 64 + ((turn * 2 + g) * 2 + way) * 3 + step

    def scatter(turn, g):
        for way in range(2):
            index = index_of(turn, g, way, 0)
            for place, to in around(way, 0):
                send(
                    partial.at[turn, chunk(g, way, place)], first_in.at[turn, g, way, places[way][0]], index, to
                )
            sent(first_in.at[turn, g, way, pl.ds(0, 3)], index)

    def summed(parts):
        squares = [part[TILES] for part in parts]
        square = (squares[0] + squares[1]) + (squares[2] + squares[3])
        norm = jnp.sqrt(square)
        inverse = 1.0 / positive(norm)
        total = jnp.zeros((TILES, 8, 128), F32)
        for part, w in zip(parts, squares):
            total = total + part[pl.ds(0, TILES)] * (jnp.sqrt(w) * inverse)
        return total, square, norm

    def middle(turn, g):
        for way in range(2):
            here, there = places[way]
            which = chunk(g, way, here)
            arrive(first_in.at[turn, g, way, pl.ds(0, 3)], index_of(turn, g, way, 0))
            parts = [partial.at[turn, which]] + [first_in.at[turn, g, way, place] for place, _ in around(way, 0)]
            total, square, _ = summed(parts)
            second_in[turn, g, way, there, pl.ds(0, TILES)] = total
            second_in[turn, g, way, there, TILES] = square
            index = index_of(turn, g, way, 1)
            for _, to in around(way, 1):
                send(second_in.at[turn, g, way, there], second_in.at[turn, g, way, there], index, to)
            sent(second_in.at[turn, g, way, pl.ds(0, 3)], index)

    def spread(turn, g):
        for way in range(2):
            here, _ = places[way]
            which = chunk(g, way, here)
            arrive(second_in.at[turn, g, way, pl.ds(0, 3)], index_of(turn, g, way, 1))
            total, square, norm = summed([second_in.at[turn, g, way, place] for place in range(4)])
            if turn == 1:
                v_norm = v_coef[0, 4 * g + 2 * way + lax.rem(here, 2)]
                total = total - right[0, which, pl.ds(0, TILES)] * (norm / v_norm)
            right[turn, which, pl.ds(0, TILES)] = total
            right[turn, which, TILES] = square
            index = index_of(turn, g, way, 2)
            for _, to in around(way, 0):
                send(right.at[turn, which], right.at[turn, which], index, to)
            sent(right.at[turn, pl.ds(0, 3)], index)

    def forward(turn, g):
        for way in range(2):
            arrive(right.at[turn, pl.ds(0, 3)], index_of(turn, g, way, 2))
        u_coef[turn, pl.ds(4 * g, 4)] = jnp.sqrt(right[turn, pl.ds(8 * g, 4), TILES])
        slabs = [(pl.ds(8 * g + 4 * (j // TILES), 4), j % TILES) for j in range(2 * TILES)]
        squares = jnp.zeros((4, 8, 128), F32)
        for h, i in slabs:
            v = right[turn, h, i]
            squares = squares + v * v
        squares = lane_sum(squares)
        twin_out[turn, g] = as_row(squares.reshape(HALF, 128))
        send(twin_out.at[turn, g], twin_in.at[turn, g], 20 + 2 * turn + g, twin)
        sent(twin_out.at[turn, g], 20 + 2 * turn + g)
        inverse = 1.0 / positive(jnp.sqrt(squares))
        first = jnp.zeros((2 * HALF, DEPTH), F32)
        second = jnp.zeros((HALF, DEPTH), F32)
        for k in range(STEPS):
            where = pl.ds(k * DEPTH, DEPTH)
            w = [(right[turn, h, i] * inverse).reshape(HALF, 128) for h, i in slabs[2 * k:2 * k + 2]]
            w_high, w_low = split(jnp.concatenate(w, axis=1))
            both = jnp.concatenate([w_high, w_low], axis=0)
            first = first + jnp.dot(both, high_turned[where, :], preferred_element_type=F32)
            second = second + jnp.dot(w_high, low_turned[where, :], preferred_element_type=F32)
        result = first[:HALF] + (first[HALF:] + second)
        for n in range(2):
            halves[turn, g, n] = result[:, 128 * n:128 * (n + 1)].reshape(4, 8, 128)
        index = 24 + 2 * turn + g
        send(halves.at[turn, g, 1 - core], half_in.at[turn, g], index, twin)
        sent(half_in.at[turn, g], index)
        arrive(twin_in.at[turn, g], 20 + 2 * turn + g)
        z_row[turn, g, z] = twin_out[turn, g] + twin_in[turn, g]
        other = as_column(twin_in[turn, g])
        inverse = 1.0 / positive(jnp.sqrt(squares + other))
        own, other = jnp.sqrt(squares) * inverse, jnp.sqrt(other) * inverse
        for to in line:
            send(z_row.at[turn, g, z], z_row.at[turn, g, z], 12 + 2 * turn + g, to)
        sent(z_row.at[turn, g, pl.ds(0, 15)], 12 + 2 * turn + g)
        arrive(half_in.at[turn, g], index)
        line_out[turn, g] = halves[turn, g, core] * own + half_in[turn, g] * other
        index = 16 + 2 * turn + g
        mine, my_eight = owned(turn, g)
        for k in range(4):
            to = owner(turn, g, k)

            @pl.when(to != z)
            def _():
                send(line_out.at[turn, g, k], line_in.at[turn, g, z], index, {"row": me, "col": 2 * to + core})

        @pl.when(mine)
        def _():
            line_in[turn, g, z] = line_out[turn, g, my_eight]

        sent(line_in.at[turn, g, pl.ds(0, 3)], index, mine)
        sent(line_in.at[turn, g, pl.ds(0, 4)], index, jnp.logical_not(mine))

    def tile_sum(turn, g):
        mine, eight = owned(turn, g)
        arrive(z_row.at[turn, g, pl.ds(0, 15)], 12 + 2 * turn + g)
        total = z_row[turn, g, 0]
        for s in range(1, 16):
            total = total + z_row[turn, g, s]
        v_coef[turn, pl.ds(4 * g, 4)] = jnp.sqrt(as_column(total))

        @pl.when(mine)
        def _():
            v_norm = v_coef[turn, 4 * g + eight]
            inverse = 1.0 / v_norm
            weights = [jnp.sqrt(as_tile(z_row[turn, g, s], eight)) * inverse for s in range(16)]
            if turn == 0:
                where = pl.ds(pl.multiple_of(HALF * g + 8 * eight, 8), 8)
                before = base[where, pl.ds(pl.multiple_of(128 * core, 128), 128)]
            else:
                before = left[g, core, eight]
            before = before * (v_norm / u_coef[turn, 4 * g + eight])
            arrive(line_in.at[turn, g, pl.ds(0, 15)], 16 + 2 * turn + g)
            tile = line_in[turn, g, 0] * weights[0]
            for s in range(1, 16):
                tile = tile + line_in[turn, g, s] * weights[s]
            tile = tile - before
            if turn == 0:
                left[g, core, eight] = tile
                for to in line:
                    send(left.at[g, core, eight], left.at[g, core, eight], 28 + g, to)
            else:
                end_xy[g, me] = tile_row(lane_sum(tile * tile), eight)
                for to in plane:
                    send(end_xy.at[g, me], end_xy.at[g, me], 60 + g, to)
        if turn == 0:
            sent(line_in.at[0, g, pl.ds(0, 15)], 28 + g, mine)
        else:
            sent(end_xy.at[g, pl.ds(0, 15)], 60 + g, mine)

    def back(g):
        mine, _ = owned(0, g)
        pl.when(mine)(lambda: arrive(left.at[g, 0, pl.ds(0, 3)], 28 + g))
        pl.when(jnp.logical_not(mine))(lambda: arrive(left.at[g, 0], 28 + g))
        send(left.at[g, core], left.at[g, core], 30 + g, twin)
        sent(left.at[g, 0], 30 + g)
        arrive(left.at[g, 0], 30 + g)
        block = [left[g, n].reshape(HALF, 128) for n in range(2)]
        x_high, both = scaled(jnp.concatenate(block, axis=1), 1, [g])
        for k in range(STEPS):
            product(x_high, both, k, 1, [g])
        scatter(1, g)

    def tile_end(g):
        mine, eight = owned(1, g)

        @pl.when(mine)
        def _():
            arrive(end_xy.at[g, pl.ds(0, 15)], 60 + g)
            total = end_xy[g, 0]
            for s in range(1, 16):
                total = total + end_xy[g, s]
            end_z[g, core, eight] = total
            for to in line:
                send(end_z.at[g, core, eight], end_z.at[g, core, eight], 62 + g, to)
            for to in other_line + [twin]:
                send(end_z.at[g, core, eight], end_z.at[g, core, eight], 32 + g, to)
        sent(end_xy.at[g, pl.ds(0, 15)], 62 + g, mine)
        sent(end_xy.at[g], 32 + g, mine)

    def combine(g):
        mine, _ = owned(1, g)
        pl.when(mine)(lambda: arrive(end_z.at[g, 0, pl.ds(0, 3)], 62 + g))
        pl.when(jnp.logical_not(mine))(lambda: arrive(end_z.at[g, 0], 62 + g))
        arrive(end_z.at[g, 0], 32 + g)
        where = pl.ds(4 * g, 4)
        phi_bar, u_first = u_coef[0, where], u_coef[1, where]
        v_first, v_second = v_coef[0, where], v_coef[1, where]
        ends = [end_z[g, n, k] for n in range(2) for k in range(4)]
        total = ends[0]
        for end in ends[1:]:
            total = total + end
        u_second = jnp.sqrt(as_column(total))
        rho = jnp.sqrt(v_first * v_first + u_first * u_first)
        cosine, sine = v_first / rho, u_first / rho
        step = cosine * phi_bar / rho
        phi_bar = sine * phi_bar
        rho_bar = -cosine * v_second
        turn_back = sine * v_second / rho
        rho = jnp.sqrt(rho_bar * rho_bar + u_second * u_second)
        step_second = (rho_bar / rho) * phi_bar / rho
        for_first = (step - step_second * turn_back) / v_first
        for_second = step_second / v_second
        for j in range(2 * TILES):
            h, i = pl.ds(8 * g + 4 * (j // TILES), 4), j % TILES
            value = right[0, h, i] * for_first + right[1, h, i] * for_second
            out[pl.ds(HALF * g, HALF), pl.ds(128 * j, 128)] = value.reshape(HALF, 128)

    def turn_over(start, stop):
        for k in range(start, stop):
            where = pl.ds(k * DEPTH, DEPTH)
            d_high, d_low = split(jnp.transpose(raw[:, where]))
            high_turned[where, :] = d_high
            low_turned[where, :] = d_low

    fetch.wait()
    x_high, both = scaled(base[...], 0, [0, 1])
    for k in range(STEPS):
        load(k).wait()
        where = pl.ds(k * DEPTH, DEPTH)
        d_high, d_low = split(raw[:, where])
        high[:, where] = d_high
        low[:, where] = d_low
        product(x_high, both, k, 0, [0, 1])
    pl.semaphore_wait(barrier, 11)
    for g in range(2):
        scatter(0, g)
    greet(0, 2)
    turn_over(0, 5)
    for g in range(2):
        middle(0, g)
    greeted(0)
    greet(1, 4)
    turn_over(5, 10)
    for g in range(2):
        spread(0, g)
    turn_over(10, STEPS)
    greeted(1)
    forward(0, 0)
    forward(0, 1)
    tile_sum(0, 0)
    tile_sum(0, 1)
    back(0)
    back(1)
    for step in (middle, spread):
        for g in range(2):
            step(1, g)
    forward(1, 0)
    forward(1, 1)
    tile_sum(1, 0)
    tile_sum(1, 1)
    tile_end(0)
    tile_end(1)
    combine(0)
    combine(1)
    for when, wait in waits:
        if when is None:
            wait()
        else:
            pl.when(when)(wait)


def local(design, targets):
    tile = (8, 128)
    return pl.pallas_call(
        kernel,
        out_shape=jax.ShapeDtypeStruct((SETS, COLS), F32),
        in_specs=[pl.BlockSpec(memory_space=pltpu.HBM)] * 2,
        out_specs=pl.BlockSpec(memory_space=pltpu.VMEM),
        scratch_shapes=[
            pltpu.VMEM((DEPTH, COLS), F32),
            pltpu.VMEM((DEPTH, COLS), BF16),
            pltpu.VMEM((DEPTH, COLS), BF16),
            pltpu.VMEM((COLS, DEPTH), BF16),
            pltpu.VMEM((COLS, DEPTH), BF16),
            pltpu.VMEM((SETS, DEPTH), F32),
            pltpu.VMEM((2, 16, 16) + tile, F32),
            pltpu.VMEM((2, 2, 2, 4, 16) + tile, F32),
            pltpu.VMEM((2, 2, 2, 4, 16) + tile, F32),
            pltpu.VMEM((2, 16, 16) + tile, F32),
            pltpu.VMEM((2, 2, 16, 1, 128), F32),
            pltpu.VMEM((2, 2, 1, 128), F32),
            pltpu.VMEM((2, 2, 1, 128), F32),
            pltpu.VMEM((2, 2, 4) + tile, F32),
            pltpu.VMEM((2, 2, 16) + tile, F32),
            pltpu.VMEM((2, 2, 2, 4) + tile, F32),
            pltpu.VMEM((2, 2, 4) + tile, F32),
            pltpu.VMEM((2, 2, 4) + tile, F32),
            pltpu.VMEM((2, 8) + tile, F32),
            pltpu.VMEM((2, 8) + tile, F32),
            pltpu.VMEM((2, 16, 1, 128), F32),
            pltpu.VMEM((2, 2, 4, 1, 128), F32),
            pltpu.SemaphoreType.DMA((STEPS + 1,)),
            pltpu.SemaphoreType.DMA((88,)),
            pltpu.SemaphoreType.DMA((88,)),
            pltpu.SemaphoreType.REGULAR((2,)),
        ],
        compiler_params=pltpu.CompilerParams(
            collective_id=0, has_side_effects=True, vmem_limit_bytes=61 << 20
        ),
    )(design, targets)


def solution(mesh):
    in_specs = (P("row", "col"), P(None, "row"))
    return jax.shard_map(local, mesh=mesh, in_specs=in_specs, out_specs=P(None, "col"), check_vma=False)
```

```python
import jax
import jax.numpy as jnp
from jax import lax
from jax.experimental import pallas as pl
from jax.experimental.pallas import tpu as pltpu
from jax.sharding import PartitionSpec as P

MESH = pl.DeviceIdType.MESH
F32 = jnp.float32
BF16 = jnp.bfloat16
SETS = 64
HALF = 32
DEPTH = 256
COLS = 3840
TILES = 15
STEPS = COLS // DEPTH
FAR_FIRST = [(2, 2), (2, 1), (2, 3), (1, 2), (3, 2), (2, 0), (0, 2), (1, 1), (3, 3), (1, 3), (3, 1), (0, 1), (0, 3), (1, 0), (3, 0)]


def split(x):
    high = x.astype(BF16)
    low = (x - high.astype(F32)).astype(BF16)
    return high, low


def lane_sum(x):
    return jnp.broadcast_to(jnp.sum(x, axis=-1, keepdims=True), x.shape)


def as_row(column):
    at = lax.broadcasted_iota(jnp.int32, (HALF, 128), 0) == lax.broadcasted_iota(jnp.int32, (HALF, 128), 1)
    return jnp.sum(jnp.where(at, column, 0.0), axis=0, keepdims=True)


def as_column(row):
    at = lax.broadcasted_iota(jnp.int32, (HALF, 128), 0) == lax.broadcasted_iota(jnp.int32, (HALF, 128), 1)
    return lane_sum(jnp.where(at, jnp.broadcast_to(row, (HALF, 128)), 0.0)).reshape(4, 8, 128)


def as_tile(row, group):
    sets = lax.broadcasted_iota(jnp.int32, (8, 128), 0) + 8 * group
    at = sets == lax.broadcasted_iota(jnp.int32, (8, 128), 1)
    return lane_sum(jnp.where(at, jnp.broadcast_to(row, (8, 128)), 0.0))


def tile_row(tile, group):
    sets = lax.broadcasted_iota(jnp.int32, (8, 128), 0) + 8 * group
    at = sets == lax.broadcasted_iota(jnp.int32, (8, 128), 1)
    return jnp.sum(jnp.where(at, tile, 0.0), axis=0, keepdims=True)


def positive(x):
    return jnp.where(x > 0.0, x, 1.0)


def kernel(
    design, targets, out,
    raw, high, low, high_turned, low_turned, base, partial, first_in, second_in, right, z_row, twin_out, twin_in, line_out, line_in,
    halves, half_in, left, v_coef, u_coef, end_xy, end_z,
    load_sem, send_sem, recv_sem, greeting,
):
    me = lax.axis_index("row")
    col = lax.axis_index("col")
    x, y = me // 4, lax.rem(me, 4)
    z, core = col // 2, lax.rem(col, 2)
    firsts = ((4, 5), (11, 12))

    def owner(turn, g, k):
        return lax.rem(firsts[turn][g] + 2 * k, 16)

    def owned(turn, g):
        ahead = lax.rem(z + 16 - firsts[turn][g], 16)
        return (ahead < 8) & (lax.rem(ahead, 2) == 0), lax.rem(ahead // 2, 4)

    def in_plane(dx, dy):
        return lax.rem(x + dx, 4), lax.rem(y + dy, 4)

    def plane_id(tx, ty):
        return {"row": tx * 4 + ty, "col": col}

    plane = [plane_id(*in_plane(*d)) for d in FAR_FIRST]
    line = [
        {"row": me, "col": lax.rem(col + 2 * d, 32)}
        for d in (8, 7, 9, 6, 10, 5, 11, 4, 12, 3, 13, 2, 14, 1, 15)
    ]
    twin = {"row": me, "col": 2 * z + 1 - core}
    other_line = [{"row": me, "col": lax.rem(2 * (z + d) + 1 - core, 32)} for d in range(1, 16)]
    on_line = {d: {"row": me, "col": lax.rem(col + 2 * d, 32)} for d in (1, 2, 4, 12, 14, 15)}
    near = [plane_id(*in_plane(d, 0)) for d in (1, 2, 3)] + [plane_id(*in_plane(0, d)) for d in (1, 2, 3)]
    near = near + [on_line[d] for d in (1, 2, 14, 15)] + [twin]

    def greet(n, distance):
        for d in (distance, 16 - distance):
            pl.semaphore_signal(greeting.at[n], inc=1, device_id=on_line[d], device_id_type=MESH)

    def greeted(n):
        pl.semaphore_wait(greeting.at[n], 2)

    waits = []

    def send(src, dst, index, to):
        pltpu.make_async_remote_copy(
            src_ref=src, dst_ref=dst, send_sem=send_sem.at[index], recv_sem=recv_sem.at[index],
            device_id=to, device_id_type=MESH,
        ).start()

    def arrive(ref, index):
        pltpu.make_async_copy(ref, ref, recv_sem.at[index]).wait()

    def sent(ref, index, when=None):
        def wait():
            pltpu.make_async_copy(ref, ref, send_sem.at[index]).wait()
        waits.append((when, wait))

    def load(k):
        where = pl.ds(k * DEPTH, DEPTH)
        return pltpu.make_async_copy(design.at[:, where], raw.at[:, where], load_sem.at[k])

    barrier = pltpu.get_barrier_semaphore()
    for to in near:
        pl.semaphore_signal(barrier, inc=1, device_id=to, device_id_type=MESH)
    fetch = pltpu.make_async_copy(targets, base, load_sem.at[STEPS])
    fetch.start()
    for k in range(STEPS):
        load(k).start()

    def scaled(block, turn, groups):
        squares = jnp.broadcast_to(jnp.sum(block * block, axis=1, keepdims=True), (block.shape[0], 128))
        for i, g in enumerate(groups):
            for h in range(2):
                partial[turn, pl.ds(8 * g + 4 * h, 4), 0] = squares[HALF * i:HALF * (i + 1)].reshape(4, 8, 128)
        norm = positive(jnp.sqrt(squares))
        norm = jnp.concatenate([norm, norm], axis=1)
        x_high, x_low = split(block / norm)
        return x_high, jnp.concatenate([x_high, x_low], axis=0)

    def product(x_high, both, k, turn, groups):
        rows = x_high.shape[0]
        where = pl.ds(k * DEPTH, DEPTH)
        first = jnp.dot(both, high[:, where], preferred_element_type=F32)
        second = jnp.dot(x_high, low[:, where], preferred_element_type=F32)
        result = first[:rows] + (first[rows:] + second)
        for i in range(2):
            h, j = divmod(2 * k + i, TILES)
            for n, g in enumerate(groups):
                partial[turn, pl.ds(8 * g + 4 * h, 4), j + 1] = (
                    result[HALF * n:HALF * (n + 1), 128 * i:128 * (i + 1)].reshape(4, 8, 128)
                )

    places = ((y, x), (x, y))

    def chunk(g, way, place):
        return 8 * g + 4 * (place // 2) + 2 * way + lax.rem(place, 2)

    def around(way, leg):
        found = []
        for d in (2, 1, 3):
            if (way == 0) == (leg == 0):
                tx, ty = x, lax.rem(y + d, 4)
                found.append((ty, plane_id(tx, ty)))
            else:
                tx, ty = lax.rem(x + d, 4), y
                found.append((tx, plane_id(tx, ty)))
        return found

    def index_of(turn, g, way, step, part):
        return 64 + (((turn * 2 + g) * 2 + way) * 3 + step) * 2 + part

    parts = (pl.ds(0, 8), pl.ds(8, 8))

    def scatter(turn, g):
        for part, where in enumerate(parts):
            for way in range(2):
                here, _ = places[way]
                index = index_of(turn, g, way, 0, part)
                for place, to in around(way, 0):
                    send(
                        partial.at[turn, chunk(g, way, place), where],
                        first_in.at[turn, g, way, here, where], index, to,
                    )
                sent(first_in.at[turn, g, way, pl.ds(0, 3), where], index)

    def summed(refs, part):
        squares = [ref[0] for ref in refs]
        square = (squares[0] + squares[1]) + (squares[2] + squares[3])
        norm = jnp.sqrt(square)
        inverse = 1.0 / positive(norm)
        weights = [jnp.sqrt(w) * inverse for w in squares]
        where = pl.ds(1, 7) if part == 0 else pl.ds(8, 8)
        total = refs[0][where] * weights[0]
        for ref, weight in zip(refs[1:], weights[1:]):
            total = total + ref[where] * weight
        return total, square, norm, where

    def middle(turn, g):
        for part in range(2):
            for way in range(2):
                here, there = places[way]
                which = chunk(g, way, here)
                arrive(first_in.at[turn, g, way, pl.ds(0, 3), parts[part]], index_of(turn, g, way, 0, part))
                refs = [partial.at[turn, which]] + [first_in.at[turn, g, way, p] for p, _ in around(way, 0)]
                total, square, _, where = summed(refs, part)
                second_in[turn, g, way, there, where] = total
                if part == 0:
                    second_in[turn, g, way, there, 0] = square
                index = index_of(turn, g, way, 1, part)
                block = second_in.at[turn, g, way, there, parts[part]]
                for _, to in around(way, 1):
                    send(block, block, index, to)
                sent(second_in.at[turn, g, way, pl.ds(0, 3), parts[part]], index)

    def spread(turn, g):
        for part in range(2):
            for way in range(2):
                here, _ = places[way]
                which = chunk(g, way, here)
                arrive(second_in.at[turn, g, way, pl.ds(0, 3), parts[part]], index_of(turn, g, way, 1, part))
                total, square, norm, where = summed([second_in.at[turn, g, way, p] for p in range(4)], part)
                if turn == 1:
                    v_norm = v_coef[0, 4 * g + 2 * way + lax.rem(here, 2)]
                    total = total - right[0, which, where] * (norm / v_norm)
                right[turn, which, where] = total
                if part == 0:
                    right[turn, which, 0] = square
                index = index_of(turn, g, way, 2, part)
                block = right.at[turn, which, parts[part]]
                for _, to in around(way, 0):
                    send(block, block, index, to)
                sent(right.at[turn, pl.ds(0, 3), parts[part]], index)

    def forward(turn, g):
        for way in range(2):
            for part in range(2):
                arrive(right.at[turn, pl.ds(0, 3), parts[part]], index_of(turn, g, way, 2, part))
        u_coef[turn, pl.ds(4 * g, 4)] = jnp.sqrt(right[turn, pl.ds(8 * g, 4), 0])
        slabs = [(pl.ds(8 * g + 4 * (j // TILES), 4), j % TILES + 1) for j in range(2 * TILES)]
        squares = jnp.zeros((4, 8, 128), F32)
        for h, i in slabs:
            v = right[turn, h, i]
            squares = squares + v * v
        squares = lane_sum(squares)
        twin_out[turn, g] = as_row(squares.reshape(HALF, 128))
        send(twin_out.at[turn, g], twin_in.at[turn, g], 20 + 2 * turn + g, twin)
        sent(twin_out.at[turn, g], 20 + 2 * turn + g)
        inverse = 1.0 / positive(jnp.sqrt(squares))
        first = jnp.zeros((2 * HALF, DEPTH), F32)
        second = jnp.zeros((HALF, DEPTH), F32)
        for k in range(STEPS):
            where = pl.ds(k * DEPTH, DEPTH)
            w = [(right[turn, h, i] * inverse).reshape(HALF, 128) for h, i in slabs[2 * k:2 * k + 2]]
            w_high, w_low = split(jnp.concatenate(w, axis=1))
            both = jnp.concatenate([w_high, w_low], axis=0)
            first = first + jnp.dot(both, high_turned[where, :], preferred_element_type=F32)
            second = second + jnp.dot(w_high, low_turned[where, :], preferred_element_type=F32)
        result = first[:HALF] + (first[HALF:] + second)
        for n in range(2):
            halves[turn, g, n] = result[:, 128 * n:128 * (n + 1)].reshape(4, 8, 128)
        index = 24 + 2 * turn + g
        send(halves.at[turn, g, 1 - core], half_in.at[turn, g], index, twin)
        sent(half_in.at[turn, g], index)
        arrive(twin_in.at[turn, g], 20 + 2 * turn + g)
        z_row[turn, g, z] = twin_out[turn, g] + twin_in[turn, g]
        other = as_column(twin_in[turn, g])
        inverse = 1.0 / positive(jnp.sqrt(squares + other))
        own, other = jnp.sqrt(squares) * inverse, jnp.sqrt(other) * inverse
        for to in line:
            send(z_row.at[turn, g, z], z_row.at[turn, g, z], 12 + 2 * turn + g, to)
        sent(z_row.at[turn, g, pl.ds(0, 15)], 12 + 2 * turn + g)
        arrive(half_in.at[turn, g], index)
        line_out[turn, g] = halves[turn, g, core] * own + half_in[turn, g] * other
        index = 16 + 2 * turn + g
        mine, my_eight = owned(turn, g)
        for k in range(4):
            to = owner(turn, g, k)

            @pl.when(to != z)
            def _():
                send(line_out.at[turn, g, k], line_in.at[turn, g, z], index, {"row": me, "col": 2 * to + core})

        @pl.when(mine)
        def _():
            line_in[turn, g, z] = line_out[turn, g, my_eight]

        sent(line_in.at[turn, g, pl.ds(0, 3)], index, mine)
        sent(line_in.at[turn, g, pl.ds(0, 4)], index, jnp.logical_not(mine))

    def tile_sum(turn, g):
        mine, eight = owned(turn, g)
        arrive(z_row.at[turn, g, pl.ds(0, 15)], 12 + 2 * turn + g)
        total = z_row[turn, g, 0]
        for s in range(1, 16):
            total = total + z_row[turn, g, s]
        v_coef[turn, pl.ds(4 * g, 4)] = jnp.sqrt(as_column(total))

        @pl.when(mine)
        def _():
            v_norm = v_coef[turn, 4 * g + eight]
            inverse = 1.0 / v_norm
            weights = [jnp.sqrt(as_tile(z_row[turn, g, s], eight)) * inverse for s in range(16)]
            if turn == 0:
                where = pl.ds(pl.multiple_of(HALF * g + 8 * eight, 8), 8)
                before = base[where, pl.ds(pl.multiple_of(128 * core, 128), 128)]
            else:
                before = left[g, core, eight]
            before = before * (v_norm / u_coef[turn, 4 * g + eight])
            arrive(line_in.at[turn, g, pl.ds(0, 15)], 16 + 2 * turn + g)
            tile = line_in[turn, g, 0] * weights[0]
            for s in range(1, 16):
                tile = tile + line_in[turn, g, s] * weights[s]
            tile = tile - before
            if turn == 0:
                left[g, core, eight] = tile
                for to in line:
                    send(left.at[g, core, eight], left.at[g, core, eight], 28 + g, to)
            else:
                end_xy[g, me] = tile_row(lane_sum(tile * tile), eight)
                for to in plane:
                    send(end_xy.at[g, me], end_xy.at[g, me], 60 + g, to)
        if turn == 0:
            sent(line_in.at[0, g, pl.ds(0, 15)], 28 + g, mine)
        else:
            sent(end_xy.at[g, pl.ds(0, 15)], 60 + g, mine)

    def back(g):
        mine, _ = owned(0, g)
        pl.when(mine)(lambda: arrive(left.at[g, 0, pl.ds(0, 3)], 28 + g))
        pl.when(jnp.logical_not(mine))(lambda: arrive(left.at[g, 0], 28 + g))
        send(left.at[g, core], left.at[g, core], 30 + g, twin)
        sent(left.at[g, 0], 30 + g)
        arrive(left.at[g, 0], 30 + g)
        block = [left[g, n].reshape(HALF, 128) for n in range(2)]
        x_high, both = scaled(jnp.concatenate(block, axis=1), 1, [g])
        for k in range(STEPS):
            product(x_high, both, k, 1, [g])
        scatter(1, g)

    def tile_end(g):
        mine, eight = owned(1, g)

        @pl.when(mine)
        def _():
            arrive(end_xy.at[g, pl.ds(0, 15)], 60 + g)
            total = end_xy[g, 0]
            for s in range(1, 16):
                total = total + end_xy[g, s]
            end_z[g, core, eight] = total
            for to in line:
                send(end_z.at[g, core, eight], end_z.at[g, core, eight], 62 + g, to)
            for to in other_line + [twin]:
                send(end_z.at[g, core, eight], end_z.at[g, core, eight], 32 + g, to)
        sent(end_xy.at[g, pl.ds(0, 15)], 62 + g, mine)
        sent(end_xy.at[g], 32 + g, mine)

    def combine(g):
        mine, _ = owned(1, g)
        pl.when(mine)(lambda: arrive(end_z.at[g, 0, pl.ds(0, 3)], 62 + g))
        pl.when(jnp.logical_not(mine))(lambda: arrive(end_z.at[g, 0], 62 + g))
        arrive(end_z.at[g, 0], 32 + g)
        where = pl.ds(4 * g, 4)
        phi_bar, u_first = u_coef[0, where], u_coef[1, where]
        v_first, v_second = v_coef[0, where], v_coef[1, where]
        ends = [end_z[g, n, k] for n in range(2) for k in range(4)]
        total = ends[0]
        for end in ends[1:]:
            total = total + end
        u_second = jnp.sqrt(as_column(total))
        rho = jnp.sqrt(v_first * v_first + u_first * u_first)
        cosine, sine = v_first / rho, u_first / rho
        step = cosine * phi_bar / rho
        phi_bar = sine * phi_bar
        rho_bar = -cosine * v_second
        turn_back = sine * v_second / rho
        rho = jnp.sqrt(rho_bar * rho_bar + u_second * u_second)
        step_second = (rho_bar / rho) * phi_bar / rho
        for_first = (step - step_second * turn_back) / v_first
        for_second = step_second / v_second
        for j in range(2 * TILES):
            h, i = pl.ds(8 * g + 4 * (j // TILES), 4), j % TILES + 1
            value = right[0, h, i] * for_first + right[1, h, i] * for_second
            out[pl.ds(HALF * g, HALF), pl.ds(128 * j, 128)] = value.reshape(HALF, 128)

    def turn_over(start, stop):
        for k in range(start, stop):
            where = pl.ds(k * DEPTH, DEPTH)
            d_high, d_low = split(jnp.transpose(raw[:, where]))
            high_turned[where, :] = d_high
            low_turned[where, :] = d_low

    fetch.wait()
    x_high, both = scaled(base[...], 0, [0, 1])
    for k in range(STEPS):
        load(k).wait()
        where = pl.ds(k * DEPTH, DEPTH)
        d_high, d_low = split(raw[:, where])
        high[:, where] = d_high
        low[:, where] = d_low
        product(x_high, both, k, 0, [0, 1])
    pl.semaphore_wait(barrier, 11)
    for g in range(2):
        scatter(0, g)
    greet(0, 2)
    turn_over(0, 5)
    for g in range(2):
        middle(0, g)
    greeted(0)
    greet(1, 4)
    turn_over(5, 10)
    for g in range(2):
        spread(0, g)
    turn_over(10, STEPS)
    greeted(1)
    forward(0, 0)
    forward(0, 1)
    tile_sum(0, 0)
    tile_sum(0, 1)
    back(0)
    back(1)
    for step in (middle, spread):
        for g in range(2):
            step(1, g)
    forward(1, 0)
    forward(1, 1)
    tile_sum(1, 0)
    tile_sum(1, 1)
    tile_end(0)
    tile_end(1)
    combine(0)
    combine(1)
    for when, wait in waits:
        if when is None:
            wait()
        else:
            pl.when(when)(wait)


def local(design, targets):
    tile = (8, 128)
    return pl.pallas_call(
        kernel,
        out_shape=jax.ShapeDtypeStruct((SETS, COLS), F32),
        in_specs=[pl.BlockSpec(memory_space=pltpu.HBM)] * 2,
        out_specs=pl.BlockSpec(memory_space=pltpu.VMEM),
        scratch_shapes=[
            pltpu.VMEM((DEPTH, COLS), F32),
            pltpu.VMEM((DEPTH, COLS), BF16),
            pltpu.VMEM((DEPTH, COLS), BF16),
            pltpu.VMEM((COLS, DEPTH), BF16),
            pltpu.VMEM((COLS, DEPTH), BF16),
            pltpu.VMEM((SETS, DEPTH), F32),
            pltpu.VMEM((2, 16, 16) + tile, F32),
            pltpu.VMEM((2, 2, 2, 4, 16) + tile, F32),
            pltpu.VMEM((2, 2, 2, 4, 16) + tile, F32),
            pltpu.VMEM((2, 16, 16) + tile, F32),
            pltpu.VMEM((2, 2, 16, 1, 128), F32),
            pltpu.VMEM((2, 2, 1, 128), F32),
            pltpu.VMEM((2, 2, 1, 128), F32),
            pltpu.VMEM((2, 2, 4) + tile, F32),
            pltpu.VMEM((2, 2, 16) + tile, F32),
            pltpu.VMEM((2, 2, 2, 4) + tile, F32),
            pltpu.VMEM((2, 2, 4) + tile, F32),
            pltpu.VMEM((2, 2, 4) + tile, F32),
            pltpu.VMEM((2, 8) + tile, F32),
            pltpu.VMEM((2, 8) + tile, F32),
            pltpu.VMEM((2, 16, 1, 128), F32),
            pltpu.VMEM((2, 2, 4, 1, 128), F32),
            pltpu.SemaphoreType.DMA((STEPS + 1,)),
            pltpu.SemaphoreType.DMA((112,)),
            pltpu.SemaphoreType.DMA((112,)),
            pltpu.SemaphoreType.REGULAR((2,)),
        ],
        compiler_params=pltpu.CompilerParams(
            collective_id=0, has_side_effects=True, vmem_limit_bytes=61 << 20
        ),
    )(design, targets)


def solution(mesh):
    in_specs = (P("row", "col"), P(None, "row"))
    return jax.shard_map(local, mesh=mesh, in_specs=in_specs, out_specs=P(None, "col"), check_vma=False)
```
